32 devices in a mesh: pat: 2 (over x), gx: 16 (over z, y, core).
Axes of the slice: x: 2, y: 2, z: 4, core: 2. Of those that a mesh axis runs over, the one named last changes fastest.
Arguments:
- pattern_index: int32 [2], P('pat'), may hold values from 0 to 7
- patterns: float32 [8, 128, 1024], P(None, 'gx'), may hold values from -6 to 6
- freq_bins: int32 [16], replicated, may hold values from 0 to 127
- absorption: float32 [128, 1024, 128], P('gx'), may hold values from 0.05 to 0.5
- forward_start: float32 [2, 128, 1024, 128], P('pat', 'gx'), may hold values from -6 to 6
- adjoint_start: float32 [2, 128, 1024, 128], P('pat', 'gx'), may hold values from -6 to 6
- measured: float32 [2, 2, 16, 1024], P('pat', None, None, 'gx'), may hold values from -6 to 6
Outputs:
- gradient: float32 [128, 1024, 128], P('gx', 'pat')
- model: float32 [2, 2, 16, 1024], P('pat', None, None, 'gx')
The draws below stay inside these ranges and needn't reach their ends.
All inputs are finite; a program needn't handle non-finite values.
Results may differ from the reference program's by a relative error of at most 0.00029.
Values sent between devices are 32-bit elements; how exact they have to be, the bound alone decides.
A program may use at most 128 MiB of HBM per device.

```python
import math
import jax
import jax.numpy as jnp
from jax import lax

GROUPS = 2
NTABLE = 8
NX = 128
NY = 1024
NZ = 128
K = 16
SWEEPS = 4


def touch_ends(result, rng, least, largest):
    longest = result.shape.index(max(result.shape))
    spots = []
    for shift in (0, 1):
        where = [jax.random.randint(jax.random.fold_in(rng, axis), (), 0, length) for axis, length in enumerate(result.shape)]
        where[longest] = (where[longest] + shift) % result.shape[longest]
        spots.append(tuple(where))
    return result.at[spots[0]].set(least).at[spots[1]].set(largest)


def level_of(rng, extent, shards, least, top_value):
    def one(axis_at, parts):
        steps = jax.random.uniform(jax.random.fold_in(jax.random.fold_in(rng, 6), axis_at), (parts,), jnp.float32, least / len(shards), top_value / len(shards))
        return jnp.repeat(jnp.exp(steps), extent[axis_at] // parts).reshape((-1,) + (1,) * (len(extent) - axis_at - 1))

    gain = one(*shards[0])
    for cut in shards[1:]:
        gain = gain * one(*cut)
    return gain


def noise(key, dims, width, most, shards=(), kind=jnp.bfloat16):
    entries = jax.random.normal(key, dims, jnp.float32) * width
    if len(shards) > 0:
        entries = level_of(key, dims, shards, -0.22, 0.18) * entries
    return jnp.clip(entries, min=-most, max=most).astype(kind)


def setup_inputs(seed: int = 0) -> dict:
    arg_keys = jax.random.split(jax.random.key(seed), 8)
    return {
        "pattern_index": jax.random.randint(arg_keys[0], (GROUPS,), 0, NTABLE).astype(jnp.int32),
        "patterns": noise(arg_keys[1], (NTABLE, NX, NY), 1.0, 6.0, ((1, 16),), jnp.float32),
        "freq_bins": touch_ends(jax.random.randint(arg_keys[2], (K,), 0, NX), jax.random.fold_in(arg_keys[2], 1), 0, NX - 1).astype(jnp.int32),
        "absorption": jnp.clip(jnp.exp(math.log(0.5) - 2.3025851 * jax.random.uniform(arg_keys[3], (NX, NY, NZ), jnp.float32) ** level_of(arg_keys[3], (NX, NY, NZ), ((0, 16),), -0.2, 0.2)), 0.05, 0.5),
        "forward_start": noise(arg_keys[4], (GROUPS, NX, NY, NZ), 1.0, 6.0, ((0, 2), (1, 16)), jnp.float32),
        "adjoint_start": noise(arg_keys[5], (GROUPS, NX, NY, NZ), 1.0, 6.0, ((0, 2), (1, 16)), jnp.float32),
        "measured": noise(arg_keys[6], (GROUPS, 2, K, NY), 1.0, 6.0, ((0, 2), (3, 16)), jnp.float32),
    }


def sweep_weight(sweep):
    return 1.0 / (1.25 + 0.75 * math.cos(math.pi * (2 * sweep + 1) / (2 * SWEEPS)))

def relaxation(start, source, diag):
    field = start
    for sweep in range(SWEEPS):
        padded = jnp.pad(field, 1)
        beside_all = padded[2:, 1:-1, 1:-1] + padded[:-2, 1:-1, 1:-1]
        beside_all = beside_all + padded[1:-1, 2:, 1:-1] + padded[1:-1, :-2, 1:-1]
        beside_all = beside_all + padded[1:-1, 1:-1, 2:] + padded[1:-1, 1:-1, :-2]
        drive = -(diag * field - beside_all)
        drive = drive.at[:, :, 0].add(source)
        field = field + sweep_weight(sweep) * drive / diag
    return field

def reference(pattern_index, patterns, freq_bins, absorption, forward_start, adjoint_start, measured):
    diag = 6.0 + absorption
    positions = jnp.arange(NX, dtype=jnp.int32)
    phase = freq_bins[:, None] * positions[None, :] % NX
    angle = 2.0 * math.pi / NX * phase.astype(jnp.float32)
    cos_table = jnp.cos(angle) / math.sqrt(NX)
    sin_table = jnp.sin(angle) / math.sqrt(NX)
    high = lax.Precision.HIGHEST

    def one_group(total, inputs):
        index, start_fwd, start_adj, data = inputs
        source = patterns[index]
        fluence = relaxation(start_fwd, source, diag)
        surface = fluence[:, :, 0]
        real_part = jnp.dot(cos_table, surface, precision=high, preferred_element_type=jnp.float32)
        imag_part = -jnp.dot(sin_table, surface, precision=high, preferred_element_type=jnp.float32)
        model = jnp.stack([real_part, imag_part])
        misfit = model - data
        adjoint_source = jnp.dot(cos_table.T, misfit[0], precision=high, preferred_element_type=jnp.float32) - jnp.dot(sin_table.T, misfit[1], precision=high, preferred_element_type=jnp.float32)
        adjoint = relaxation(start_adj, adjoint_source, diag)
        return (total - fluence * adjoint, model)
    initial = jnp.zeros((NX, NY, NZ), jnp.float32)
    gradient, model = lax.scan(one_group, initial, (pattern_index, forward_start, adjoint_start, measured))
    return (gradient, model)
```

```python
import functools
import math

import jax
import jax.numpy as jnp
from jax import lax
from jax.experimental import pallas as pl
from jax.experimental.pallas import tpu as pltpu
from jax.sharding import PartitionSpec as P

SWEEPS = 4
EDGE = 8
LANES = 128
MESH = pl.DeviceIdType.MESH


def sweep_weight(sweep):
    return 1.0 / (1.25 + 0.75 * math.cos(math.pi * (2 * sweep + 1) / (2 * SWEEPS)))


def make_tables(freq_bins, positions, total_x):
    phase = freq_bins[:, None] * positions[None, :] % total_x
    angle = 2.0 * math.pi / total_x * phase.astype(jnp.float32)
    return (jnp.cos(angle) / math.sqrt(total_x), jnp.sin(angle) / math.sqrt(total_x))


def chunk_rows(rows):
    tiles = rows // 8
    for size in range(min(tiles, 13), 0, -1):
        if tiles % size == 0:
            return size * 8
    return 8


def solve_kernel(
    count, planes, ny, depth,
    fwd, adj, absorb, fsrc, asrc, out,
    buf, inv, srcs, gsend, grecv,
    load_sems, send_sems, recv_sems, gsend_sems, grecv_sems,
):
    half = ny // 2
    span = half + EDGE
    me = lax.axis_index("gx")
    pat = lax.axis_index("pat")
    last = count - 1
    has_low = jnp.where(me > 0, 1, 0)
    has_high = jnp.where(me < last, 1, 0)

    first_row = (
        pl.multiple_of((1 - pat) * (half - EDGE), 8),
        pl.multiple_of(pat * (half - EDGE), 8),
    )
    skip = (pl.multiple_of((1 - pat) * EDGE, 8), pl.multiple_of(pat * EDGE, 8))

    loads = []
    for part in range(2):
        rows = pl.ds(first_row[part], span)
        inner = (pl.ds(1, planes), pl.ds(8, span))
        group = (
            pltpu.make_async_copy(
                fwd.at[:, rows], buf.at[(part, 0, 0) + inner], load_sems.at[part, 0]
            ),
            pltpu.make_async_copy(
                adj.at[:, rows], buf.at[(part, 1, 0) + inner], load_sems.at[part, 1]
            ),
            pltpu.make_async_copy(absorb.at[:, rows], inv.at[part], load_sems.at[part, 2]),
            pltpu.make_async_copy(fsrc.at[rows], srcs.at[part, 0], load_sems.at[part, 3]),
            pltpu.make_async_copy(asrc.at[rows], srcs.at[part, 1], load_sems.at[part, 4]),
        )
        for copy in group:
            copy.start()
        loads.append(group)

    barrier = pltpu.get_barrier_semaphore()
    pl.semaphore_signal(barrier, inc=1, device_id={"pat": 1 - pat}, device_id_type=MESH)

    @pl.when(me > 0)
    def _():
        pl.semaphore_signal(barrier, inc=1, device_id={"gx": me - 1}, device_id_type=MESH)

    @pl.when(me < last)
    def _():
        pl.semaphore_signal(barrier, inc=1, device_id={"gx": me + 1}, device_id_type=MESH)

    edge_rows = jnp.zeros((8, depth), jnp.float32)

    def clear_edges(i, _):
        part, field, slot, plane = i // (4 * planes), i // (2 * planes) % 2, i // planes % 2, i % planes
        buf[part, field, slot, plane + 1, 0:8] = edge_rows
        buf[part, field, slot, plane + 1, 8 + span : 16 + span] = edge_rows
        return 0

    lax.fori_loop(0, 8 * planes, clear_edges, 0)

    def clear_plane(plane):
        def body(i, _):
            buf[i // 4, i // 2 % 2, i % 2, plane] = jnp.zeros((16 + span, depth), jnp.float32)
            return 0

        lax.fori_loop(0, 8, body, 0)

    @pl.when(me == 0)
    def _():
        clear_plane(0)

    @pl.when(me == last)
    def _():
        clear_plane(planes + 1)

    pl.semaphore_wait(barrier, 1 + has_low + has_high)

    rows_held = pl.ds(8, span)

    def face(part, field, sweep, side):
        slot = sweep % 2
        return pltpu.make_async_remote_copy(
            src_ref=buf.at[part, field, slot, 1 if side == 0 else planes, rows_held],
            dst_ref=buf.at[part, field, slot, planes + 1 if side == 0 else 0, rows_held],
            send_sem=send_sems.at[part, field, sweep, side],
            recv_sem=recv_sems.at[part, field, sweep, side],
            device_id={"gx": me - 1 if side == 0 else me + 1},
            device_id_type=MESH,
        )

    def send_faces(part, field, sweep):
        @pl.when(me > 0)
        def _():
            face(part, field, sweep, 0).start()

        @pl.when(me < last)
        def _():
            face(part, field, sweep, 1).start()

    def wait_sent(part, field, sweep):
        @pl.when(me > 0)
        def _():
            face(part, field, sweep, 0).wait_send()

        @pl.when(me < last)
        def _():
            face(part, field, sweep, 1).wait_send()

    def wait_faces(part, field, sweep):
        @pl.when(me > 0)
        def _():
            face(part, field, sweep, 1).wait_recv()

        @pl.when(me < last)
        def _():
            face(part, field, sweep, 0).wait_recv()

    def invert(part):
        step = chunk_rows(span)

        def body(plane, _):
            for at in range(0, span, step):
                inv[part, plane, at : at + step] = 1.0 / (6.0 + inv[part, plane, at : at + step])
            return 0

        lax.fori_loop(0, planes, body, 0)

    for field in range(2):
        loads[0][field].wait()
        send_faces(0, field, 0)
    for copy in loads[0][2:]:
        copy.wait()
    invert(0)
    for copy in loads[1]:
        copy.wait()
    invert(1)

    step_rows = chunk_rows(span)
    lane = lax.broadcasted_iota(jnp.int32, (step_rows, depth), 1)
    top = lane == 0
    bottom = lane == depth - 1

    def update(part, field, sweep, plane, weight):
        now, later = sweep % 2, (sweep + 1) % 2
        at_now = (part, field, now)
        for at in range(0, span, step_rows):
            here = pl.ds(8 + at, step_rows)
            center = buf[part, field, now, plane, here]
            column = srcs[part, field, pl.ds(at, step_rows)]
            column = pltpu.roll(column, lax.rem(depth + 1 - plane, depth), 1)
            beside = buf[part, field, now, plane - 1, here] + buf[part, field, now, plane + 1, here]
            beside = beside + buf[part, field, now, plane, pl.ds(7 + at, step_rows)]
            beside = beside + buf[part, field, now, plane, pl.ds(9 + at, step_rows)]
            beside = beside + jnp.where(top, column, pltpu.roll(center, 1, 1))
            beside = beside + jnp.where(bottom, 0.0, pltpu.roll(center, depth - 1, 1))
            scale = inv[part, plane - 1, pl.ds(at, step_rows)]
            buf[part, field, later, plane, here] = center + weight * (beside * scale - center)

    def one_step(index, _):
        field = index % 2
        stage = index // 2
        part, sweep = stage // SWEEPS, stage % SWEEPS
        weight = jnp.float32(sweep_weight(0))
        for other in range(1, SWEEPS):
            weight = jnp.where(sweep == other, jnp.float32(sweep_weight(other)), weight)
        wait_faces(part, field, sweep)

        @pl.when(sweep > 0)
        def _():
            wait_sent(part, field, sweep - 1)

        def outer(i, _):
            update(part, field, sweep, 1 + i * (planes - 1), weight)
            return 0

        lax.fori_loop(0, 2, outer, 0)
        coming = stage + 1

        @pl.when(coming < 2 * SWEEPS)
        def _():
            send_faces(coming // SWEEPS, field, coming % SWEEPS)

        def within(plane, _):
            update(part, field, sweep, plane, weight)
            return 0

        lax.fori_loop(2, planes, within, 0)
        return 0

    def terms(part, plane, at, rows):
        where = pl.ds(8 + skip[part] + at, rows)
        slot = SWEEPS % 2
        return -(buf[part, 0, slot, plane + 1, where] * buf[part, 1, slot, plane + 1, where])

    term_rows = chunk_rows(half)

    def swap(plane):
        return pltpu.make_async_remote_copy(
            src_ref=gsend.at[plane],
            dst_ref=grecv.at[plane],
            send_sem=gsend_sems.at[plane],
            recv_sem=grecv_sems.at[plane],
            device_id={"pat": 1 - pat},
            device_id_type=MESH,
        )

    lax.fori_loop(0, 2 * SWEEPS, one_step, 0)

    def give(plane, _):
        for at in range(0, half, term_rows):
            gsend[plane, at : at + term_rows] = terms(0, plane, at, term_rows)
        swap(plane).start()
        return 0

    lax.fori_loop(0, planes, give, 0)

    lax.fori_loop(2 * SWEEPS, 4 * SWEEPS, one_step, 0)

    def finish(plane, _):
        swap(plane).wait_recv()
        for at in range(0, half, term_rows):
            out[plane, at : at + term_rows] = (
                terms(1, plane, at, term_rows) + grecv[plane, at : at + term_rows]
            )
        swap(plane).wait_send()
        return 0

    lax.fori_loop(0, planes, finish, 0)
    for part in range(2):
        for field in range(2):
            wait_sent(part, field, SWEEPS - 1)


def solve_both(fwd, adj, absorb, fsrc, asrc):
    planes, ny, depth = absorb.shape
    half = ny // 2
    span = half + EDGE
    count = lax.axis_size("gx")
    f32 = jnp.float32
    return pl.pallas_call(
        functools.partial(solve_kernel, count, planes, ny, depth),
        out_shape=jax.ShapeDtypeStruct((planes, half, depth), f32),
        in_specs=[pl.BlockSpec(memory_space=pl.ANY)] * 5,
        out_specs=pl.BlockSpec(memory_space=pltpu.VMEM),
        scratch_shapes=[
            pltpu.VMEM((2, 2, 2, planes + 2, span + 16, depth), f32),
            pltpu.VMEM((2, planes, span, depth), f32),
            pltpu.VMEM((2, 2, span, LANES), f32),
            pltpu.VMEM((planes, half, depth), f32),
            pltpu.VMEM((planes, half, depth), f32),
            pltpu.SemaphoreType.DMA((2, 5)),
            pltpu.SemaphoreType.DMA((2, 2, SWEEPS, 2)),
            pltpu.SemaphoreType.DMA((2, 2, SWEEPS, 2)),
            pltpu.SemaphoreType.DMA((planes,)),
            pltpu.SemaphoreType.DMA((planes,)),
        ],
        compiler_params=pltpu.CompilerParams(
            collective_id=0, has_side_effects=True, vmem_limit_bytes=48 * 1024 * 1024
        ),
        cost_estimate=pl.CostEstimate(
            flops=24 * SWEEPS * planes * ny * depth,
            bytes_accessed=14 * planes * ny * depth,
            transcendentals=0,
        ),
    )(fwd, adj, absorb, fsrc, asrc)


def surface_field(start, absorb, source):
    deep = SWEEPS + 1
    count = lax.axis_size("gx")
    top = jnp.transpose(start[:, :, :deep], (0, 2, 1))
    scale = 1.0 / (6.0 + jnp.transpose(absorb[:, :, :deep], (0, 2, 1)))
    packed = jnp.concatenate([top, scale, source[:, None, :]], axis=1)
    forward = [(i, i + 1) for i in range(count - 1)]
    backward = [(target, origin) for origin, target in forward]
    low = lax.ppermute(packed[-SWEEPS:], "gx", forward)
    high = lax.ppermute(packed[:SWEEPS], "gx", backward)
    packed = jnp.concatenate([low, packed, high], axis=0)
    field, scale, drive = packed[:, :deep], packed[:, deep : 2 * deep], packed[:, 2 * deep :]
    drive = jnp.pad(drive, ((0, 0), (0, deep - 1), (0, 0)))
    for sweep in range(SWEEPS):
        side = jnp.pad(field, 1)
        beside = side[2:, 1:-1, 1:-1] + side[:-2, 1:-1, 1:-1]
        beside = beside + side[1:-1, 1:-1, 2:] + side[1:-1, 1:-1, :-2]
        beside = beside + side[1:-1, 2:, 1:-1] + side[1:-1, :-2, 1:-1]
        field = field + sweep_weight(sweep) * ((beside + drive) * scale - field)
    return field[SWEEPS:-SWEEPS, 0]


def shards(pattern_index, patterns, freq_bins, absorption, forward_start, adjoint_start, measured):
    high = lax.Precision.HIGHEST
    planes = forward_start.shape[1]
    total_x = lax.axis_size("gx") * planes
    bins = freq_bins.shape[0]
    source = lax.dynamic_index_in_dim(patterns, pattern_index[0], 0, keepdims=False)
    surface = surface_field(forward_start[0], absorption, source)
    columns = lax.all_to_all(surface, "gx", split_axis=1, concat_axis=0, tiled=True)
    cos_table, sin_table = make_tables(freq_bins, jnp.arange(total_x, dtype=jnp.int32), total_x)
    table = jnp.concatenate([cos_table, -sin_table], axis=0)
    model = jnp.dot(table, columns, precision=high)
    misfit = model - measured[0].reshape(2 * bins, -1)
    back = lax.dot_general(misfit, table, (((0,), (0,)), ((), ())), precision=high)
    drive = lax.all_to_all(back, "gx", split_axis=1, concat_axis=0, tiled=True)
    widen = ((0, 0), (0, LANES - planes))
    gradient = solve_both(
        forward_start[0],
        adjoint_start[0],
        absorption,
        jnp.pad(source.T, widen),
        jnp.pad(drive, widen),
    )
    return (gradient, model.reshape(measured.shape))


def solution(mesh):
    placed = (
        P("pat"),
        P(None, "gx", None),
        P(),
        P("gx", None, None),
        P("pat", "gx", None, None),
        P("pat", "gx", None, None),
        P("pat", None, None, "gx"),
    )
    return jax.shard_map(
        shards,
        mesh=mesh,
        in_specs=placed,
        out_specs=(P("gx", "pat", None), P("pat", None, None, "gx")),
        check_vma=False,
    )
```

```python
import functools
import math

import jax
import jax.numpy as jnp
from jax import lax
from jax.experimental import pallas as pl
from jax.experimental.pallas import tpu as pltpu
from jax.sharding import PartitionSpec as P

SWEEPS = 4
EDGE = 8
LANES = 128
MESH = pl.DeviceIdType.MESH


def sweep_weight(sweep):
    return 1.0 / (1.25 + 0.75 * math.cos(math.pi * (2 * sweep + 1) / (2 * SWEEPS)))


def make_tables(freq_bins, positions, total_x):
    phase = freq_bins[:, None] * positions[None, :] % total_x
    angle = 2.0 * math.pi / total_x * phase.astype(jnp.float32)
    return (jnp.cos(angle) / math.sqrt(total_x), jnp.sin(angle) / math.sqrt(total_x))


def chunk_rows(rows):
    tiles = rows // 8
    for size in range(min(tiles, 13), 0, -1):
        if tiles % size == 0:
            return size * 8
    return 8


def solve_kernel(
    count, planes, ny, depth,
    fwd, adj, absorb, fsrc, pattern, measured, table, own_table, out, model,
    buf, inv, srcs, given, layer, other_layer, surfaces, images, modelled, drive,
    load_sems, send_sems, recv_sems, give_send, give_recv, layer_send, layer_recv,
    all_send, all_recv, pat_send, pat_recv,
):
    half = ny // 2
    span = half + EDGE
    width = ny // count
    me = lax.axis_index("gx")
    pat = lax.axis_index("pat")
    last = count - 1

    first_row = (
        pl.multiple_of((1 - pat) * (half - EDGE), 8),
        pl.multiple_of(pat * (half - EDGE), 8),
    )
    skip = (pl.multiple_of((1 - pat) * EDGE, 8), pl.multiple_of(pat * EDGE, 8))
    half_at = (pl.multiple_of((1 - pat) * half, LANES), pl.multiple_of(pat * half, LANES))
    inner = (pl.ds(1, planes), pl.ds(8, span))

    loads = []
    for part in range(2):
        rows = pl.ds(first_row[part], span)
        group = (
            pltpu.make_async_copy(
                fwd.at[:, rows], buf.at[(part, 0, 0) + inner], load_sems.at[part, 0]
            ),
            pltpu.make_async_copy(absorb.at[:, rows], inv.at[part], load_sems.at[part, 1]),
            pltpu.make_async_copy(fsrc.at[rows], srcs.at[part, 0], load_sems.at[part, 2]),
        )
        for copy in group:
            copy.start()
        loads.append(group)
    adj_load = pltpu.make_async_copy(
        adj.at[:, pl.ds(first_row[1], span)], buf.at[(1, 1, 0) + inner], load_sems.at[1, 3]
    )
    adj_load.start()

    barrier = pltpu.get_barrier_semaphore()
    pl.semaphore_signal(barrier, inc=1, device_id={"pat": 1 - pat}, device_id_type=MESH)

    def greet(step, _):
        other = lax.rem(me + step, count)
        pl.semaphore_signal(barrier, inc=1, device_id={"gx": other}, device_id_type=MESH)
        return 0

    lax.fori_loop(1, count, greet, 0)

    edge_rows = jnp.zeros((8, depth), jnp.float32)

    def clear_edges(i, _):
        part, field, slot, plane = i // (4 * planes), i // (2 * planes) % 2, i // planes % 2, i % planes
        buf[part, field, slot, plane + 1, 0:8] = edge_rows
        buf[part, field, slot, plane + 1, 8 + span : 16 + span] = edge_rows
        return 0

    lax.fori_loop(0, 8 * planes, clear_edges, 0)

    def clear_plane(plane, layer_at):
        def body(i, _):
            buf[i // 4, i // 2 % 2, i % 2, plane] = jnp.zeros((16 + span, depth), jnp.float32)
            return 0

        lax.fori_loop(0, 8, body, 0)

        def layers(i, _):
            layer[i % 2, layer_at + i // 2] = jnp.zeros((8, ny), jnp.float32)
            return 0

        lax.fori_loop(0, 2 * SWEEPS, layers, 0)

    @pl.when(me == 0)
    def _():
        clear_plane(0, 0)

    @pl.when(me == last)
    def _():
        clear_plane(planes + 1, SWEEPS + planes)

    images[me] = measured[...]
    pl.semaphore_wait(barrier, count)

    rows_held = pl.ds(8, span)

    def face(part, field, sweep, side):
        slot = sweep % 2
        return pltpu.make_async_remote_copy(
            src_ref=buf.at[part, field, slot, 1 if side == 0 else planes, rows_held],
            dst_ref=buf.at[part, field, slot, planes + 1 if side == 0 else 0, rows_held],
            send_sem=send_sems.at[part, field, sweep, side],
            recv_sem=recv_sems.at[part, field, sweep, side],
            device_id={"gx": me - 1 if side == 0 else me + 1},
            device_id_type=MESH,
        )

    def layers_to(which, side):
        return pltpu.make_async_remote_copy(
            src_ref=layer.at[which, pl.ds(SWEEPS if side == 0 else planes, SWEEPS)],
            dst_ref=layer.at[which, pl.ds(SWEEPS + planes if side == 0 else 0, SWEEPS)],
            send_sem=layer_send.at[which, side],
            recv_sem=layer_recv.at[which, side],
            device_id={"gx": me - 1 if side == 0 else me + 1},
            device_id_type=MESH,
        )

    def by_side(low, high):
        @pl.when(me > 0)
        def _():
            low()

        @pl.when(me < last)
        def _():
            high()

    def send_faces(part, field, sweep):
        by_side(
            lambda: face(part, field, sweep, 0).start(), lambda: face(part, field, sweep, 1).start()
        )

    def wait_sent(part, field, sweep):
        by_side(
            lambda: face(part, field, sweep, 0).wait_send(),
            lambda: face(part, field, sweep, 1).wait_send(),
        )

    def wait_faces(part, field, sweep):
        by_side(
            lambda: face(part, field, sweep, 1).wait_recv(),
            lambda: face(part, field, sweep, 0).wait_recv(),
        )

    def to_all(kind, block, step, sender):
        return pltpu.make_async_remote_copy(
            src_ref=block.at[sender],
            dst_ref=block.at[sender],
            send_sem=all_send.at[kind, step],
            recv_sem=all_recv.at[kind, sender],
            device_id={"gx": lax.rem(me + step, count)},
            device_id_type=MESH,
        )

    def spread(kind, block):
        def body(step, _):
            to_all(kind, block, step, me).start()
            return 0

        lax.fori_loop(1, count, body, 0)

    def collect(kind, block):
        def body(step, _):
            to_all(kind, block, step, lax.rem(me + count - step, count)).wait_recv()
            to_all(kind, block, step, me).wait_send()
            return 0

        lax.fori_loop(1, count, body, 0)

    def to_pattern(src, dst, sem):
        return pltpu.make_async_remote_copy(
            src_ref=src,
            dst_ref=dst,
            send_sem=pat_send.at[sem],
            recv_sem=pat_recv.at[sem],
            device_id={"pat": 1 - pat},
            device_id_type=MESH,
        )

    start_swap = to_pattern(
        adj.at[:, pl.ds(first_row[0], span)], buf.at[(0, 1, 0) + inner], 0
    )
    drive_swap = to_pattern(drive.at[pl.ds(first_row[0], span)], srcs.at[0, 1], 1)

    def give(plane):
        return pltpu.make_async_remote_copy(
            src_ref=buf.at[0, 0, SWEEPS % 2, plane + 1, pl.ds(8 + skip[0], half)],
            dst_ref=given.at[plane],
            send_sem=give_send.at[plane],
            recv_sem=give_recv.at[plane],
            device_id={"pat": 1 - pat},
            device_id_type=MESH,
        )

    step_rows = chunk_rows(span)

    def invert(part):
        def body(plane, _):
            for at in range(0, span, step_rows):
                inv[part, plane, at : at + step_rows] = 1.0 / (
                    6.0 + inv[part, plane, at : at + step_rows]
                )
            return 0

        lax.fori_loop(0, planes, body, 0)

    for part in range(2):
        loads[part][0].wait()
        if part == 0:
            send_faces(0, 0, 0)
            start_swap.start()
        for copy in loads[part][1:]:
            copy.wait()
        invert(part)

    pick = (
        lax.broadcasted_iota(jnp.int32, (8, depth), 0)
        == lax.broadcasted_iota(jnp.int32, (8, depth), 1)
    ).astype(jnp.float32)
    high = lax.Precision.HIGHEST
    over_lanes = (((1,), (1,)), ((), ()))

    def lift(plane, _):
        for part in range(2):
            lanes = pl.ds(half_at[part], half)
            block = buf[part, 0, 0, plane + 1, pl.ds(8 + skip[part], half)]
            layer[0, SWEEPS + plane, :, lanes] = lax.dot_general(
                pick, block, over_lanes, precision=high, preferred_element_type=jnp.float32
            )
            block = inv[part, plane, pl.ds(skip[part], half)]
            layer[1, SWEEPS + plane, :, lanes] = lax.dot_general(
                pick, block, over_lanes, precision=high, preferred_element_type=jnp.float32
            )
        layer[1, SWEEPS + plane, 7:8] = pattern[pl.ds(plane, 1)]
        return 0

    lax.fori_loop(0, planes, lift, 0)
    for which in range(2):
        by_side(lambda: layers_to(which, 0).start(), lambda: layers_to(which, 1).start())
    send_faces(1, 0, 0)
    spread(0, images)
    adj_load.wait()

    lane = lax.broadcasted_iota(jnp.int32, (step_rows, depth), 1)
    top = lane == 0
    bottom = lane == depth - 1

    def update(part, field, sweep, plane, weight):
        now, later = sweep % 2, (sweep + 1) % 2
        scales = jnp.maximum(part, field)
        for at in range(0, span, step_rows):
            here = pl.ds(8 + at, step_rows)
            center = buf[part, field, now, plane, here]
            column = srcs[part, field, pl.ds(at, step_rows)]
            column = pltpu.roll(column, lax.rem(depth + 1 - plane, depth), 1)
            beside = buf[part, field, now, plane - 1, here] + buf[part, field, now, plane + 1, here]
            beside = beside + buf[part, field, now, plane, pl.ds(7 + at, step_rows)]
            beside = beside + buf[part, field, now, plane, pl.ds(9 + at, step_rows)]
            beside = beside + jnp.where(top, column, pltpu.roll(center, 1, 1))
            beside = beside + jnp.where(bottom, 0.0, pltpu.roll(center, depth - 1, 1))
            scale = inv[scales, plane - 1, pl.ds(at, step_rows)]
            buf[part, field, later, plane, here] = center + weight * (beside * scale - center)

    def one_step(index, _):
        part = index % 2
        stage = index // 2
        field, sweep = stage // SWEEPS, stage % SWEEPS
        weight = jnp.float32(sweep_weight(0))
        for other in range(1, SWEEPS):
            weight = jnp.where(sweep == other, jnp.float32(sweep_weight(other)), weight)
        wait_faces(part, field, sweep)

        @pl.when(sweep > 0)
        def _():
            wait_sent(part, field, sweep - 1)

        def outer(i, _):
            update(part, field, sweep, 1 + i * (planes - 1), weight)
            return 0

        lax.fori_loop(0, 2, outer, 0)
        coming = stage + 1

        @pl.when(index == 2 * (SWEEPS - 1))
        def _():
            start_swap.wait_recv()

        @pl.when(coming < 2 * SWEEPS)
        def _():
            send_faces(part, coming // SWEEPS, coming % SWEEPS)

        def within(plane, _):
            update(part, field, sweep, plane, weight)
            return 0

        lax.fori_loop(2, planes, within, 0)
        return 0

    lax.fori_loop(0, 2, one_step, 0)

    for which in range(2):
        by_side(lambda: layers_to(which, 1).wait_recv(), lambda: layers_to(which, 0).wait_recv())
        by_side(lambda: layers_to(which, 0).wait_send(), lambda: layers_to(which, 1).wait_send())
    row_of = lax.broadcasted_iota(jnp.int32, (8, ny), 0)
    place = lax.broadcasted_iota(jnp.int32, (8, ny), 1)

    def shallow(source, target, weight):
        def body(plane, _):
            center = source[plane]
            scale = layer[1, plane]
            beside = source[plane - 1] + source[plane + 1]
            beside = beside + jnp.where(place == 0, 0.0, pltpu.roll(center, 1, 1))
            beside = beside + jnp.where(place == ny - 1, 0.0, pltpu.roll(center, ny - 1, 1))
            beside = beside + jnp.where(row_of == 0, pltpu.roll(scale, 1, 0), pltpu.roll(center, 1, 0))
            beside = beside + pltpu.roll(center, 7, 0)
            target[plane] = center + weight * (beside * scale - center)
            return 0

        return body

    for sweep in range(SWEEPS):
        ends = (layer.at[0], other_layer)
        lax.fori_loop(
            1 + sweep,
            planes + 2 * SWEEPS - 1 - sweep,
            shallow(ends[sweep % 2], ends[(sweep + 1) % 2], sweep_weight(sweep)),
            0,
        )
    for plane in range(planes):
        surfaces[me, plane : plane + 1] = layer[0, SWEEPS + plane, 0:1]
    spread(1, surfaces)

    lax.fori_loop(2, 4, one_step, 0)

    collect(0, images)
    collect(1, surfaces)
    block_rows = max(LANES, width)
    senders = block_rows // width

    def transform(i, _):
        at = pl.multiple_of(i * block_rows, block_rows)
        strip = surfaces[:, :, pl.ds(at, block_rows)].reshape(count * planes, block_rows)
        image = jnp.dot(
            strip.T, table[...], precision=high, preferred_element_type=jnp.float32
        )
        modelled[pl.ds(at, block_rows)] = image
        misfit = image - images[pl.ds(i * senders, senders)].reshape(block_rows, LANES)
        drive[pl.ds(at, block_rows)] = jnp.dot(
            misfit, own_table[...], precision=high, preferred_element_type=jnp.float32
        )
        return 0

    lax.fori_loop(0, ny // block_rows, transform, 0)
    drive_swap.start()
    model[...] = modelled[pl.ds(pl.multiple_of(me * width, width), width)]
    srcs[1, 1] = drive[pl.ds(first_row[1], span)]

    lax.fori_loop(4, 2 * SWEEPS, one_step, 0)
    for plane in range(planes):
        give(plane).start()
    drive_swap.wait_recv()
    lax.fori_loop(2 * SWEEPS, 4 * SWEEPS, one_step, 0)

    term_rows = chunk_rows(half)
    slot = SWEEPS % 2

    def finish(plane, _):
        give(plane).wait_recv()
        for at in range(0, half, term_rows):
            where = pl.ds(8 + skip[1] + at, term_rows)
            ours = buf[1, 0, slot, plane + 1, where] * buf[1, 1, slot, plane + 1, where]
            theirs = given[plane, pl.ds(at, term_rows)] * buf[0, 1, slot, plane + 1, where]
            out[plane, at : at + term_rows] = -(ours + theirs)
        give(plane).wait_send()
        return 0

    lax.fori_loop(0, planes, finish, 0)
    start_swap.wait_send()
    drive_swap.wait_send()
    for part in range(2):
        for field in range(2):
            wait_sent(part, field, SWEEPS - 1)


def solve_both(fwd, adj, absorb, fsrc, pattern, measured, table, own_table):
    planes, ny, depth = absorb.shape
    half = ny // 2
    span = half + EDGE
    count = lax.axis_size("gx")
    f32 = jnp.float32
    dma = pltpu.SemaphoreType.DMA
    return pl.pallas_call(
        functools.partial(solve_kernel, count, planes, ny, depth),
        out_shape=(
            jax.ShapeDtypeStruct((planes, half, depth), f32),
            jax.ShapeDtypeStruct((ny // count, LANES), f32),
        ),
        in_specs=[pl.BlockSpec(memory_space=pl.ANY)] * 4
        + [pl.BlockSpec(memory_space=pltpu.VMEM)] * 4,
        out_specs=[pl.BlockSpec(memory_space=pltpu.VMEM)] * 2,
        scratch_shapes=[
            pltpu.VMEM((2, 2, 2, planes + 2, span + 16, depth), f32),
            pltpu.VMEM((2, planes, span, depth), f32),
            pltpu.VMEM((2, 2, span, LANES), f32),
            pltpu.VMEM((planes, half, depth), f32),
            pltpu.VMEM((2, planes + 2 * SWEEPS, 8, ny), f32),
            pltpu.VMEM((planes + 2 * SWEEPS, 8, ny), f32),
            pltpu.VMEM((count, planes, ny), f32),
            pltpu.VMEM((count, ny // count, LANES), f32),
            pltpu.VMEM((ny, LANES), f32),
            pltpu.VMEM((ny, LANES), f32),
            dma((2, 4)),
            dma((2, 2, SWEEPS, 2)),
            dma((2, 2, SWEEPS, 2)),
            dma((planes,)),
            dma((planes,)),
            dma((2, 2)),
            dma((2, 2)),
            dma((2, count)),
            dma((2, count)),
            dma((2,)),
            dma((2,)),
        ],
        compiler_params=pltpu.CompilerParams(
            collective_id=0, has_side_effects=True, vmem_limit_bytes=48 * 1024 * 1024
        ),
        cost_estimate=pl.CostEstimate(
            flops=24 * SWEEPS * planes * ny * depth,
            bytes_accessed=14 * planes * ny * depth,
            transcendentals=0,
        ),
    )(fwd, adj, absorb, fsrc, pattern, measured, table, own_table)


def shards(pattern_index, patterns, freq_bins, absorption, forward_start, adjoint_start, measured):
    planes = forward_start.shape[1]
    total_x = lax.axis_size("gx") * planes
    bins = freq_bins.shape[0]
    source = lax.dynamic_index_in_dim(patterns, pattern_index[0], 0, keepdims=False)
    positions = jnp.arange(total_x, dtype=jnp.int32)
    cos_table, sin_table = make_tables(freq_bins, positions, total_x)
    table = jnp.concatenate([cos_table, -sin_table], axis=0)
    table = jnp.pad(table, ((0, LANES - 2 * bins), (0, 0)))
    own_table = lax.dynamic_slice_in_dim(table, lax.axis_index("gx") * planes, planes, axis=1)
    widen = ((0, 0), (0, LANES - planes))
    gradient, model = solve_both(
        forward_start[0],
        adjoint_start[0],
        absorption,
        jnp.pad(source.T, widen),
        source,
        jnp.pad(measured[0].reshape(2 * bins, -1).T, ((0, 0), (0, LANES - 2 * bins))),
        table.T,
        jnp.pad(own_table, widen),
    )
    return (gradient, model[:, : 2 * bins].T.reshape(measured.shape))


def solution(mesh):
    placed = (
        P("pat"),
        P(None, "gx", None),
        P(),
        P("gx", None, None),
        P("pat", "gx", None, None),
        P("pat", "gx", None, None),
        P("pat", None, None, "gx"),
    )
    return jax.shard_map(
        shards,
        mesh=mesh,
        in_specs=placed,
        out_specs=(P("gx", "pat", None), P("pat", None, None, "gx")),
        check_vma=False,
    )
```

```python
import functools
import math

import jax
import jax.numpy as jnp
from jax import lax
from jax.experimental import pallas as pl
from jax.experimental.pallas import tpu as pltpu
from jax.sharding import PartitionSpec as P

SWEEPS = 4
EDGE = 8
LANES = 128
MESH = pl.DeviceIdType.MESH


def sweep_weight(sweep):
    return 1.0 / (1.25 + 0.75 * math.cos(math.pi * (2 * sweep + 1) / (2 * SWEEPS)))


def make_tables(freq_bins, positions, total_x):
    phase = freq_bins[:, None] * positions[None, :] % total_x
    angle = 2.0 * math.pi / total_x * phase.astype(jnp.float32)
    return (jnp.cos(angle) / math.sqrt(total_x), jnp.sin(angle) / math.sqrt(total_x))


def solve_kernel(
    count, planes, ny, depth,
    fwd, adj, absorb, fsrc, pattern, measured, table, own_table, out, model,
    buf, inv, srcs, given, layer, other_layer, surfaces, images, modelled, drive,
    load_sems, send_sems, recv_sems, give_send, give_recv, layer_send, layer_recv,
    all_send, all_recv, pat_send, pat_recv,
):
    half = ny // 2
    span = half + EDGE
    width = ny // count
    me = lax.axis_index("gx")
    pat = lax.axis_index("pat")
    last = count - 1

    first_row = (
        pl.multiple_of((1 - pat) * (half - EDGE), 8),
        pl.multiple_of(pat * (half - EDGE), 8),
    )
    skip = (pl.multiple_of((1 - pat) * EDGE, 8), pl.multiple_of(pat * EDGE, 8))
    half_at = (pl.multiple_of((1 - pat) * half, LANES), pl.multiple_of(pat * half, LANES))
    inner = (pl.ds(1, planes), pl.ds(8, span))

    loads = []
    for part in range(2):
        rows = pl.ds(first_row[part], span)
        group = (
            pltpu.make_async_copy(
                fwd.at[:, rows], buf.at[(part, 0, 0) + inner], load_sems.at[part, 0]
            ),
            pltpu.make_async_copy(absorb.at[:, rows], inv.at[part], load_sems.at[part, 1]),
            pltpu.make_async_copy(fsrc.at[rows], srcs.at[part, 0], load_sems.at[part, 2]),
        )
        for copy in group:
            copy.start()
        loads.append(group)
    adj_load = pltpu.make_async_copy(
        adj.at[:, pl.ds(first_row[1], span)], buf.at[(1, 1, 0) + inner], load_sems.at[1, 3]
    )
    adj_load.start()

    barrier = pltpu.get_barrier_semaphore()
    pl.semaphore_signal(barrier, inc=1, device_id={"pat": 1 - pat}, device_id_type=MESH)

    def greet(step, _):
        other = lax.rem(me + step, count)
        pl.semaphore_signal(barrier, inc=1, device_id={"gx": other}, device_id_type=MESH)
        return 0

    lax.fori_loop(1, count, greet, 0)

    edge_rows = jnp.zeros((8, depth), jnp.float32)

    def clear_edges(i, _):
        part, field, slot, plane = i // (4 * planes), i // (2 * planes) % 2, i // planes % 2, i % planes
        buf[part, field, slot, plane + 1, 0:8] = edge_rows
        buf[part, field, slot, plane + 1, 8 + span : 16 + span] = edge_rows
        return 0

    lax.fori_loop(0, 8 * planes, clear_edges, 0)

    def clear_plane(plane, layer_at):
        def body(i, _):
            buf[i // 4, i // 2 % 2, i % 2, plane] = jnp.zeros((16 + span, depth), jnp.float32)
            return 0

        lax.fori_loop(0, 8, body, 0)

        def layers(i, _):
            layer[i % 2, layer_at + i // 2] = jnp.zeros((8, ny), jnp.float32)
            return 0

        lax.fori_loop(0, 2 * SWEEPS, layers, 0)

    @pl.when(me == 0)
    def _():
        clear_plane(0, 0)

    @pl.when(me == last)
    def _():
        clear_plane(planes + 1, SWEEPS + planes)

    images[me] = measured[...]
    pl.semaphore_wait(barrier, count)

    rows_held = pl.ds(8, span)

    def face(part, field, sweep, side):
        slot = sweep % 2
        return pltpu.make_async_remote_copy(
            src_ref=buf.at[part, field, slot, 1 if side == 0 else planes, rows_held],
            dst_ref=buf.at[part, field, slot, planes + 1 if side == 0 else 0, rows_held],
            send_sem=send_sems.at[part, field, sweep, side],
            recv_sem=recv_sems.at[part, field, sweep, side],
            device_id={"gx": me - 1 if side == 0 else me + 1},
            device_id_type=MESH,
        )

    def layers_to(which, side):
        return pltpu.make_async_remote_copy(
            src_ref=layer.at[which, pl.ds(SWEEPS if side == 0 else planes, SWEEPS)],
            dst_ref=layer.at[which, pl.ds(SWEEPS + planes if side == 0 else 0, SWEEPS)],
            send_sem=layer_send.at[which, side],
            recv_sem=layer_recv.at[which, side],
            device_id={"gx": me - 1 if side == 0 else me + 1},
            device_id_type=MESH,
        )

    def by_side(low, high):
        @pl.when(me > 0)
        def _():
            low()

        @pl.when(me < last)
        def _():
            high()

    def send_faces(part, field, sweep):
        by_side(
            lambda: face(part, field, sweep, 0).start(), lambda: face(part, field, sweep, 1).start()
        )

    def wait_sent(part, field, sweep):
        by_side(
            lambda: face(part, field, sweep, 0).wait_send(),
            lambda: face(part, field, sweep, 1).wait_send(),
        )

    def wait_faces(part, field, sweep):
        by_side(
            lambda: face(part, field, sweep, 1).wait_recv(),
            lambda: face(part, field, sweep, 0).wait_recv(),
        )

    def to_all(kind, block, step, sender):
        return pltpu.make_async_remote_copy(
            src_ref=block.at[sender],
            dst_ref=block.at[sender],
            send_sem=all_send.at[kind, step],
            recv_sem=all_recv.at[kind, sender],
            device_id={"gx": lax.rem(me + step, count)},
            device_id_type=MESH,
        )

    def spread(kind, block):
        def body(step, _):
            to_all(kind, block, step, me).start()
            return 0

        lax.fori_loop(1, count, body, 0)

    def collect(kind, block):
        def body(step, _):
            to_all(kind, block, step, lax.rem(me + count - step, count)).wait_recv()
            to_all(kind, block, step, me).wait_send()
            return 0

        lax.fori_loop(1, count, body, 0)

    def to_pattern(src, dst, sem):
        return pltpu.make_async_remote_copy(
            src_ref=src,
            dst_ref=dst,
            send_sem=pat_send.at[sem],
            recv_sem=pat_recv.at[sem],
            device_id={"pat": 1 - pat},
            device_id_type=MESH,
        )

    start_swap = to_pattern(
        adj.at[:, pl.ds(first_row[0], span)], buf.at[(0, 1, 0) + inner], 0
    )
    drive_swap = to_pattern(drive.at[pl.ds(first_row[0], span)], srcs.at[0, 1], 1)

    def give(plane):
        return pltpu.make_async_remote_copy(
            src_ref=buf.at[0, 0, SWEEPS % 2, plane + 1, pl.ds(8 + skip[0], half)],
            dst_ref=given.at[plane],
            send_sem=give_send.at[plane],
            recv_sem=give_recv.at[plane],
            device_id={"pat": 1 - pat},
            device_id_type=MESH,
        )

    step_rows = span

    def invert(part):
        def body(plane, _):
            for at in range(0, span, step_rows):
                inv[part, plane, at : at + step_rows] = 1.0 / (
                    6.0 + inv[part, plane, at : at + step_rows]
                )
            return 0

        lax.fori_loop(0, planes, body, 0)

    for part in range(2):
        loads[part][0].wait()
        if part == 0:
            send_faces(0, 0, 0)
            start_swap.start()
        for copy in loads[part][1:]:
            copy.wait()
        invert(part)

    high = lax.Precision.HIGHEST
    group = LANES // 8
    eighth = lax.broadcasted_iota(jnp.int32, (LANES, depth), 1) // 8

    def lift(i, _):
        for part in range(2):
            at = pl.multiple_of(i * LANES, LANES)
            pieces = [(0, plane) for plane in range(planes)] + [(1, plane) for plane in range(planes)]
            for begin in range(0, len(pieces), group):
                packed = jnp.zeros((LANES, depth), jnp.float32)
                for spot, (which, plane) in enumerate(pieces[begin : begin + group]):
                    if which == 0:
                        block = buf[part, 0, 0, plane + 1, pl.ds(8 + skip[part] + at, LANES)]
                    else:
                        block = inv[part, plane, pl.ds(skip[part] + at, LANES)]
                    if spot > 0:
                        block = pltpu.roll(block, 8 * spot, 1)
                    packed = jnp.where(eighth == spot, block, packed)
                turned = packed.T
                for spot, (which, plane) in enumerate(pieces[begin : begin + group]):
                    layer[which, SWEEPS + plane, :, pl.ds(half_at[part] + at, LANES)] = turned[
                        8 * spot : 8 * spot + 8
                    ]
        return 0

    send_faces(1, 0, 0)
    lax.fori_loop(0, half // LANES, lift, 0)
    for plane in range(planes):
        layer[1, SWEEPS + plane, 7:8] = pattern[plane : plane + 1]
    for which in range(2):
        by_side(lambda: layers_to(which, 0).start(), lambda: layers_to(which, 1).start())
    spread(0, images)
    adj_load.wait()

    lane = lax.broadcasted_iota(jnp.int32, (step_rows, depth), 1)
    top = lane == 0
    bottom = lane == depth - 1

    def update(part, field, sweep, plane, weight):
        now, later = sweep % 2, (sweep + 1) % 2
        scales = jnp.maximum(part, field)
        for at in range(0, span, step_rows):
            here = pl.ds(8 + at, step_rows)
            center = buf[part, field, now, plane, here]
            column = srcs[part, field, pl.ds(at, step_rows)]
            column = pltpu.roll(column, lax.rem(depth + 1 - plane, depth), 1)
            beside = buf[part, field, now, plane - 1, here] + buf[part, field, now, plane + 1, here]
            beside = beside + buf[part, field, now, plane, pl.ds(7 + at, step_rows)]
            beside = beside + buf[part, field, now, plane, pl.ds(9 + at, step_rows)]
            beside = beside + jnp.where(top, column, pltpu.roll(center, 1, 1))
            beside = beside + jnp.where(bottom, 0.0, pltpu.roll(center, depth - 1, 1))
            scale = inv[scales, plane - 1, pl.ds(at, step_rows)]
            buf[part, field, later, plane, here] = center + weight * (beside * scale - center)

    def one_step(index, _):
        part = index % 2
        stage = index // 2
        field, sweep = stage // SWEEPS, stage % SWEEPS
        weight = jnp.float32(sweep_weight(0))
        for other in range(1, SWEEPS):
            weight = jnp.where(sweep == other, jnp.float32(sweep_weight(other)), weight)
        wait_faces(part, field, sweep)

        @pl.when(sweep > 0)
        def _():
            wait_sent(part, field, sweep - 1)

        def outer(i, _):
            update(part, field, sweep, 1 + i * (planes - 1), weight)
            return 0

        lax.fori_loop(0, 2, outer, 0)
        coming = stage + 1

        @pl.when(index == 2 * (SWEEPS - 1))
        def _():
            start_swap.wait_recv()

        @pl.when(coming < 2 * SWEEPS)
        def _():
            send_faces(part, coming // SWEEPS, coming % SWEEPS)

        def within(plane, _):
            update(part, field, sweep, plane, weight)
            return 0

        lax.fori_loop(2, planes, within, 0)
        return 0

    lax.fori_loop(0, 2, one_step, 0)

    for which in range(2):
        by_side(lambda: layers_to(which, 1).wait_recv(), lambda: layers_to(which, 0).wait_recv())
        by_side(lambda: layers_to(which, 0).wait_send(), lambda: layers_to(which, 1).wait_send())
    row_of = lax.broadcasted_iota(jnp.int32, (8, ny), 0)
    place = lax.broadcasted_iota(jnp.int32, (8, ny), 1)

    def shallow(sweep):
        ends = (layer.at[0], other_layer)
        source, target = ends[sweep % 2], ends[(sweep + 1) % 2]
        first, stop = 1 + sweep, planes + 2 * SWEEPS - 1 - sweep
        pair = 2 if (stop - first) % 2 == 0 else 1

        def body(i, _):
            fresh = []
            for plane in [first + i * pair + more for more in range(pair)]:
                center = source[plane]
                scale = layer[1, plane]
                beside = source[plane - 1] + source[plane + 1]
                beside = beside + jnp.where(place == 0, 0.0, pltpu.roll(center, 1, 1))
                beside = beside + jnp.where(place == ny - 1, 0.0, pltpu.roll(center, ny - 1, 1))
                beside = beside + jnp.where(
                    row_of == 0, pltpu.roll(scale, 1, 0), pltpu.roll(center, 1, 0)
                )
                beside = beside + pltpu.roll(center, 7, 0)
                fresh.append((plane, center + sweep_weight(sweep) * (beside * scale - center)))
            for plane, value in fresh:
                target[plane] = value
            return 0

        lax.fori_loop(0, (stop - first) // pair, body, 0)

    for sweep in range(SWEEPS // 2):
        shallow(sweep)
    lax.fori_loop(2, 3, one_step, 0)
    for sweep in range(SWEEPS // 2, SWEEPS):
        shallow(sweep)
    for plane in range(planes):
        surfaces[me, plane : plane + 1] = layer[0, SWEEPS + plane, 0:1]
    spread(1, surfaces)

    lax.fori_loop(3, 6, one_step, 0)

    collect(0, images)
    collect(1, surfaces)
    block_rows = max(LANES, width)
    senders = block_rows // width

    def transform(i, _):
        at = pl.multiple_of(i * block_rows, block_rows)
        strip = surfaces[:, :, pl.ds(at, block_rows)].reshape(count * planes, block_rows)
        image = jnp.dot(
            strip.T, table[...], precision=high, preferred_element_type=jnp.float32
        )
        modelled[pl.ds(at, block_rows)] = image
        misfit = image - images[pl.ds(i * senders, senders)].reshape(block_rows, LANES)
        drive[pl.ds(at, block_rows)] = jnp.dot(
            misfit, own_table[...], precision=high, preferred_element_type=jnp.float32
        )
        return 0

    lax.fori_loop(0, ny // block_rows, transform, 0)
    drive_swap.start()
    model[...] = modelled[pl.ds(pl.multiple_of(me * width, width), width)]
    srcs[1, 1] = drive[pl.ds(first_row[1], span)]

    lax.fori_loop(6, 2 * SWEEPS, one_step, 0)
    for plane in range(planes):
        give(plane).start()
    drive_swap.wait_recv()
    lax.fori_loop(2 * SWEEPS, 4 * SWEEPS, one_step, 0)

    term_rows = half
    slot = SWEEPS % 2

    def finish(plane, _):
        give(plane).wait_recv()
        for at in range(0, half, term_rows):
            where = pl.ds(8 + skip[1] + at, term_rows)
            ours = buf[1, 0, slot, plane + 1, where] * buf[1, 1, slot, plane + 1, where]
            theirs = given[plane, pl.ds(at, term_rows)] * buf[0, 1, slot, plane + 1, where]
            out[plane, at : at + term_rows] = -(ours + theirs)
        give(plane).wait_send()
        return 0

    lax.fori_loop(0, planes, finish, 0)
    start_swap.wait_send()
    drive_swap.wait_send()
    for part in range(2):
        for field in range(2):
            wait_sent(part, field, SWEEPS - 1)


def solve_both(fwd, adj, absorb, fsrc, pattern, measured, table, own_table):
    planes, ny, depth = absorb.shape
    half = ny // 2
    span = half + EDGE
    count = lax.axis_size("gx")
    f32 = jnp.float32
    dma = pltpu.SemaphoreType.DMA
    return pl.pallas_call(
        functools.partial(solve_kernel, count, planes, ny, depth),
        out_shape=(
            jax.ShapeDtypeStruct((planes, half, depth), f32),
            jax.ShapeDtypeStruct((ny // count, LANES), f32),
        ),
        in_specs=[pl.BlockSpec(memory_space=pl.ANY)] * 4
        + [pl.BlockSpec(memory_space=pltpu.VMEM)] * 4,
        out_specs=[pl.BlockSpec(memory_space=pltpu.VMEM)] * 2,
        scratch_shapes=[
            pltpu.VMEM((2, 2, 2, planes + 2, span + 16, depth), f32),
            pltpu.VMEM((2, planes, span, depth), f32),
            pltpu.VMEM((2, 2, span, LANES), f32),
            pltpu.VMEM((planes, half, depth), f32),
            pltpu.VMEM((2, planes + 2 * SWEEPS, 8, ny), f32),
            pltpu.VMEM((planes + 2 * SWEEPS, 8, ny), f32),
            pltpu.VMEM((count, planes, ny), f32),
            pltpu.VMEM((count, ny // count, LANES), f32),
            pltpu.VMEM((ny, LANES), f32),
            pltpu.VMEM((ny, LANES), f32),
            dma((2, 4)),
            dma((2, 2, SWEEPS, 2)),
            dma((2, 2, SWEEPS, 2)),
            dma((planes,)),
            dma((planes,)),
            dma((2, 2)),
            dma((2, 2)),
            dma((2, count)),
            dma((2, count)),
            dma((2,)),
            dma((2,)),
        ],
        compiler_params=pltpu.CompilerParams(
            collective_id=0, has_side_effects=True, vmem_limit_bytes=48 * 1024 * 1024
        ),
        cost_estimate=pl.CostEstimate(
            flops=24 * SWEEPS * planes * ny * depth,
            bytes_accessed=14 * planes * ny * depth,
            transcendentals=0,
        ),
    )(fwd, adj, absorb, fsrc, pattern, measured, table, own_table)


def shards(pattern_index, patterns, freq_bins, absorption, forward_start, adjoint_start, measured):
    planes = forward_start.shape[1]
    total_x = lax.axis_size("gx") * planes
    bins = freq_bins.shape[0]
    source = lax.dynamic_index_in_dim(patterns, pattern_index[0], 0, keepdims=False)
    positions = jnp.arange(total_x, dtype=jnp.int32)
    cos_table, sin_table = make_tables(freq_bins, positions, total_x)
    table = jnp.concatenate([cos_table, -sin_table], axis=0)
    table = jnp.pad(table, ((0, LANES - 2 * bins), (0, 0)))
    own_table = lax.dynamic_slice_in_dim(table, lax.axis_index("gx") * planes, planes, axis=1)
    widen = ((0, 0), (0, LANES - planes))
    gradient, model = solve_both(
        forward_start[0],
        adjoint_start[0],
        absorption,
        jnp.pad(source.T, widen),
        source,
        jnp.pad(measured[0].reshape(2 * bins, -1).T, ((0, 0), (0, LANES - 2 * bins))),
        table.T,
        jnp.pad(own_table, widen),
    )
    return (gradient, model[:, : 2 * bins].T.reshape(measured.shape))


def solution(mesh):
    placed = (
        P("pat"),
        P(None, "gx", None),
        P(),
        P("gx", None, None),
        P("pat", "gx", None, None),
        P("pat", "gx", None, None),
        P("pat", None, None, "gx"),
    )
    return jax.shard_map(
        shards,
        mesh=mesh,
        in_specs=placed,
        out_specs=(P("gx", "pat", None), P("pat", None, None, "gx")),
        check_vma=False,
    )
```
